1024 devices in a mesh: dp: 16 (over x, y), seq: 64 (over z, core).
Axes of the slice: x: 4, y: 4, z: 32, core: 2. Of those that a mesh axis runs over, the one named last changes fastest.
Arguments:
- section_input: bfloat16 [16, 32768, 384], P('dp', 'seq'), may hold values from -42 to 42
- kernel: bfloat16 [384, 5, 384], P('seq'), may hold values from -0.125 to 0.125
- cotangent: bfloat16 [16, 32768, 384], P('dp', 'seq'), may hold values from -16 to 16
Outputs:
- block_output: bfloat16 [16, 32768, 384], P('dp', 'seq')
- input_grad: bfloat16 [16, 32768, 384], P('dp', 'seq')
- kernel_grad: float32 [384, 5, 384], P('seq')
The draws below stay inside these ranges and needn't reach their ends.
All inputs are finite; a program needn't handle non-finite values.
Results may differ from the reference program's by a relative error of at most 0.0065.
Values may be sent and summed in bfloat16 or wider, within the bound.
No kernel may reach another device: no remote copies, remote signals or barrier semaphores. Data moves between devices by JAX's collectives and lax.ppermute only.
A program may use at most 32 MiB of HBM per device.

```python
import math
import jax
import jax.numpy as jnp
from jax import lax

C = 384
KW = 5
ROWS = 32768
SEQS = 16


def draw_section_input(key, part):
    noise_key, row_key, column_key = jax.random.split(key, 3)
    full_shape = (SEQS, ROWS, C)
    noise_part = jnp.clip(jax.random.normal(noise_key, full_shape, jnp.float32), -4.0, 4.0)
    log_lower = math.log(0.32)
    log_upper = math.log(3.2)
    row_scale = jnp.exp(jax.random.uniform(row_key, (SEQS, ROWS, 1), jnp.float32, log_lower, log_upper))
    column_scale = jnp.exp(jax.random.uniform(column_key, (1, 1, C), jnp.float32, log_lower, log_upper))
    return (noise_part * row_scale * column_scale).astype(jnp.bfloat16)


def spiked(array, key, source, target, parts, factor):
    def block_of(dim):
        return (jnp.arange(array.shape[dim]) // (array.shape[dim] // parts)).reshape((-1,) + (1,) * (array.ndim - 1 - dim))

    first = jax.random.permutation(key, parts)[block_of(target)]
    other_side = (block_of(target) + parts // 2) % parts
    return jnp.where((block_of(source) == first) | (block_of(source) == other_side), factor * array, array)


def levels(rng, dims, shards, low, top_value):
    factor_of, own = 1.0, jax.random.fold_in(rng, 6)
    for axis_at, parts in shards:
        heights = jnp.exp(jax.random.uniform(jax.random.fold_in(own, axis_at), (parts,), jnp.float32, low / len(shards), top_value / len(shards)))
        factor_of = factor_of * jnp.repeat(heights, dims[axis_at] // parts).reshape([-1 if axis == axis_at else 1 for axis in range(len(dims))])
    return factor_of


def noise(own_key, shape, scale, bound, shards=(), kind=jnp.bfloat16):
    entries = jax.random.normal(own_key, shape, jnp.float32) * scale
    if len(shards) > 0:
        entries = levels(own_key, shape, shards, -0.22, 0.18) * entries
    return jnp.clip(entries, min=-bound, max=bound).astype(kind)


def noise_with(key, extent, spread, limit, cuts, heavy, kind=jnp.bfloat16):
    drawn = spread * jax.random.normal(key, extent, jnp.float32)
    if cuts:
        drawn = drawn * levels(key, extent, cuts, -0.22, 0.18)
    return jnp.clip(spiked(drawn, jax.random.fold_in(key, 3), *heavy), -limit, limit).astype(kind)


def setup_inputs(seed: int = 0) -> dict:
    keys = jax.random.split(jax.random.key(seed), 4)
    return {
        "section_input": draw_section_input(jax.random.fold_in(keys[3], 71), 0),
        "kernel": noise(keys[1], (C, KW, C), (KW * C) ** -0.5, 0.125, ((0, 64),)),
        "cotangent": noise_with(keys[2], (SEQS, ROWS, C), 1.0, 16.0, ((0, 16), (1, 64)), (1, 2, 64, 4.0)),
    }


def gelu_value(values):
    return 0.5 * values * (1.0 + jax.scipy.special.erf(values * 0.7071067811865476))

def gelu_slope(values):
    cumulative = 0.5 * (1.0 + jax.scipy.special.erf(values * 0.7071067811865476))
    return cumulative + values * jnp.exp(-0.5 * values * values) * 0.3989422804014327

def reference(section_input, kernel, cotangent):
    inputs = section_input.astype(jnp.float32)
    seq_count, length, width = inputs.shape
    half_width = (KW - 1) // 2
    scale = jnp.sqrt(lax.optimization_barrier(jnp.mean(inputs * inputs, axis=-1, keepdims=True)) + 1e-05)
    normed = inputs / scale
    act = gelu_value(normed).astype(jnp.bfloat16)
    padded = jnp.pad(act, ((0, 0), (half_width, half_width), (0, 0)))
    grad_pad = jnp.pad(cotangent, ((0, 0), (half_width, half_width), (0, 0)))
    grad_flat = cotangent.reshape(seq_count * length, width)
    branch = jnp.zeros((seq_count * length, width), jnp.float32)
    act_grad = jnp.zeros((seq_count * length, width), jnp.float32)
    kernel_rows = []
    for shift in range(KW):
        window = padded[:, shift:shift + length, :].reshape(seq_count * length, width)
        branch = branch + lax.dot_general(window, kernel[:, shift, :], (((1,), (1,)), ((), ())), preferred_element_type=jnp.float32)
        kernel_rows.append(lax.dot_general(grad_flat, window, (((0,), (0,)), ((), ())), preferred_element_type=jnp.float32))
        back = grad_pad[:, 2 * half_width - shift:2 * half_width - shift + length, :].reshape(seq_count * length, width)
        act_grad = act_grad + jnp.dot(back, kernel[:, shift, :], preferred_element_type=jnp.float32)
    branch = branch.astype(jnp.bfloat16).reshape(seq_count, length, width)
    block_output = (inputs + branch.astype(jnp.float32)).astype(jnp.bfloat16)
    kernel_grad = jnp.stack(kernel_rows, axis=1) / SEQS
    act_grad = act_grad.reshape(seq_count, length, width)
    normed_grad = act_grad * gelu_slope(normed)
    project = lax.optimization_barrier(jnp.mean(normed_grad * normed, axis=-1, keepdims=True))
    input_grad = (cotangent.astype(jnp.float32) + (normed_grad - normed * project) / scale).astype(jnp.bfloat16)
    return (block_output, input_grad, kernel_grad)
```

```python
import jax
import jax.numpy as jnp
from jax import lax
from jax.sharding import Mesh, PartitionSpec as P

XY = ("x", "y")
SEQ = ("z", "core")
BF = jnp.bfloat16
F32 = jnp.float32


def gelu_value(values):
    return 0.5 * values * (1.0 + jax.scipy.special.erf(values * 0.7071067811865476))


def gelu_slope(values):
    cumulative = 0.5 * (1.0 + jax.scipy.special.erf(values * 0.7071067811865476))
    return cumulative + values * jnp.exp(-0.5 * values * values) * 0.3989422804014327


def norm(rows):
    inputs = rows.astype(F32)
    scale = jnp.sqrt(jnp.mean(inputs * inputs, axis=-1, keepdims=True) + 1e-05)
    return inputs, scale, inputs / scale


def order_matrix(width, depth, core):
    half, rest = width // 2, width // (4 * depth)
    j = lax.broadcasted_iota(jnp.int32, (width, width), 1)
    o = lax.broadcasted_iota(jnp.int32, (width, width), 0)
    side = j // half
    within = j % half
    pair = within // (2 * depth)
    place = (within // 2) % depth
    member = j % 2
    source = (place * 2 + (side + core) % 2) * (2 * rest) + 2 * pair + member
    return (o == source).astype(BF)


def local(section_input, kernel, cotangent):
    rows_in = section_input[0]
    out_grad = cotangent[0]
    length, width = rows_in.shape
    held, taps, _ = kernel.shape
    edge = (taps - 1) // 2
    depth = lax.axis_size("z")
    groups = lax.axis_size(XY)
    count = lax.axis_size(SEQ)
    pairs = held // 2
    blocks = taps * pairs
    half = width // 2
    core = lax.axis_index("core")
    spot = lax.axis_index(XY)

    by_block = kernel.reshape(pairs, 2, taps, width).transpose(2, 0, 1, 3).reshape(blocks, 2, width)
    mine = lax.dynamic_index_in_dim(by_block, jnp.minimum(spot, blocks - 1), 0, keepdims=False)
    along_z = lax.all_to_all(jnp.broadcast_to(mine, (depth, 2, width)), "z", 0, 0)
    along_z = along_z.reshape(2 * depth, width)
    own_half = lax.all_to_all(jnp.broadcast_to(along_z, (groups, 2 * depth, width)), XY, 0, 0)
    own_half = own_half[:blocks].reshape(taps, half, width)
    swap = [(0, 1), (1, 0)]
    other_half = lax.ppermute(own_half, "core", swap)
    weights = jnp.concatenate([own_half, other_half], axis=1)

    both = jnp.stack([rows_in, out_grad])
    before = lax.ppermute(both[:, length - edge :], SEQ, [(i, i + 1) for i in range(count - 1)])
    after = lax.ppermute(both[:, :edge], SEQ, [(i + 1, i) for i in range(count - 1)])
    padded_in = jnp.concatenate([before[0], rows_in, after[0]], axis=0)
    padded_grad = jnp.concatenate([before[1], out_grad, after[1]], axis=0)
    inputs, scale, normed = norm(padded_in)
    act = gelu_value(normed).astype(BF)
    inputs, scale, normed = (v[edge : edge + length] for v in (inputs, scale, normed))
    order = order_matrix(width, depth, core)
    grouped = jnp.dot(padded_grad, order, preferred_element_type=F32).astype(BF)

    centre = grouped[edge : edge + length]
    parts = jnp.stack(
        [
            lax.dot_general(
                centre,
                act[shift : shift + length],
                (((0,), (0,)), ((), ())),
                preferred_element_type=F32,
            )
            for shift in range(taps)
        ]
    )
    got = lax.ppermute(parts[:, half:].astype(BF), "core", swap)
    chip = (parts[:, :half] + got.astype(F32)).astype(BF).reshape(blocks, 2 * depth, width)
    chip = jnp.pad(chip, ((0, groups - blocks), (0, 0), (0, 0)))
    plane = lax.all_to_all(chip, XY, 0, 0)
    plane = sum(plane[i].astype(F32) for i in range(groups)).astype(BF).reshape(depth, 2, width)
    line = lax.all_to_all(plane, "z", 0, 0)
    line = jnp.sum(line.astype(F32), axis=0) / (groups * section_input.shape[0])
    full = lax.all_to_all(jnp.broadcast_to(line, (groups, 2, width)), XY, 0, 0)
    kernel_grad = (
        full[:blocks].reshape(taps, pairs, 2, width).transpose(1, 2, 0, 3).reshape(held, taps, width)
    )

    total = jnp.zeros((length, width), F32)
    carry = jnp.zeros((length, width), F32)
    for shift in range(taps):
        total = total + lax.dot_general(
            act[shift : shift + length],
            weights[shift],
            (((1,), (1,)), ((), ())),
            preferred_element_type=F32,
        )
        begin = 2 * edge - shift
        carry = carry + jnp.dot(
            grouped[begin : begin + length], weights[shift], preferred_element_type=F32
        )
    branch = lax.dot_general(
        total.astype(BF), order, (((1,), (1,)), ((), ())), preferred_element_type=F32
    )
    block_output = (inputs + branch).astype(BF)
    normed_grad = carry * gelu_slope(normed)
    project = jnp.mean(normed_grad * normed, axis=-1, keepdims=True)
    input_grad = (out_grad.astype(F32) + (normed_grad - normed * project) / scale).astype(BF)
    return (block_output[None], input_grad[None], kernel_grad)


def solution(mesh):
    seq = mesh.shape["seq"]
    side = int(round(mesh.shape["dp"] ** 0.5))
    fine = Mesh(mesh.devices.reshape(side, side, seq // 2, 2), XY + SEQ)
    return jax.shard_map(
        local,
        mesh=fine,
        in_specs=(P(XY, SEQ, None), P(SEQ, None, None), P(XY, SEQ, None)),
        out_specs=(P(XY, SEQ, None), P(XY, SEQ, None), P(SEQ, None, None)),
        check_vma=False,
    )
```

```python
import functools

import jax
import jax.numpy as jnp
from jax import lax
from jax.experimental import pallas as pl
from jax.experimental.pallas import tpu as pltpu
from jax.sharding import Mesh, PartitionSpec as P

XY = ("x", "y")
SEQ = ("z", "core")
BF = jnp.bfloat16
F32 = jnp.float32
TOP = 8
VMEM_BYTES = 24 * 1024 * 1024


def call(body, out_shape, flops, bytes_accessed, scalars=0, plain=0, scratch=()):
    specs = [pl.BlockSpec(memory_space=pltpu.SMEM)] * scalars
    specs += [pl.BlockSpec(memory_space=pltpu.VMEM)] * plain
    outs = jax.tree.map(lambda _: pl.BlockSpec(memory_space=pltpu.VMEM), out_shape)
    return pl.pallas_call(
        body,
        out_shape=out_shape,
        in_specs=specs,
        out_specs=outs,
        scratch_shapes=list(scratch),
        compiler_params=pltpu.CompilerParams(vmem_limit_bytes=VMEM_BYTES),
        cost_estimate=pl.CostEstimate(
            flops=flops, bytes_accessed=bytes_accessed, transcendentals=0
        ),
    )


def norm(rows):
    inputs = rows.astype(F32)
    scale = jnp.sqrt(jnp.mean(inputs * inputs, axis=-1, keepdims=True) + 1e-05)
    return inputs, scale, inputs / scale


def cumulative(values):
    return 0.5 * (1.0 + lax.erf(values * 0.7071067811865476))


def gelu_rows(rows):
    normed = norm(rows)[2]
    return (normed * cumulative(normed)).astype(BF)


def order_rows(core, width, depth):
    half = width // 2
    held = width // (2 * depth)
    j = lax.broadcasted_iota(jnp.int32, (width, 1), 0)
    side = (j >= half).astype(jnp.int32)
    within = j - side * half
    pair = within // (2 * depth)
    member = (within // depth) % 2
    place = within % depth
    source = (place * 2 + (side + core) % 2) * held + 2 * pair + member
    o = lax.broadcasted_iota(jnp.int32, (width, width), 1)
    return jnp.where(o == source, 1.0, 0.0).astype(BF)


def turn(a, b):
    return lax.dot_general(a, b, (((1,), (1,)), ((), ())), preferred_element_type=F32)


def act_body(depth, core_ref, x_ref, g_ref, act_ref, cot_t_ref):
    order = order_rows(core_ref[0], x_ref.shape[1], depth)
    cot_t_ref[...] = turn(order, g_ref[...]).astype(BF)
    act_ref[...] = gelu_rows(x_ref[...])


def grad_body(taps, act_ref, cot_t_ref, before_ref, after_ref, mine_ref, other_ref, pad_ref):
    length, width = act_ref.shape
    edge = (taps - 1) // 2
    half = width // 2
    pad_ref[TOP - edge : TOP] = gelu_rows(before_ref[...]).astype(F32)
    pad_ref[TOP : TOP + length] = act_ref[...].astype(F32)
    pad_ref[TOP + length : TOP + length + edge] = gelu_rows(after_ref[...]).astype(F32)
    cot_t = cot_t_ref[...]
    for shift in range(taps):
        begin = TOP - edge + shift
        window = pad_ref[begin : begin + length].astype(BF)
        part = jnp.dot(cot_t, window, preferred_element_type=F32)
        mine_ref[shift] = part[:half]
        other_ref[shift] = part[half:].astype(BF)


def slope_body(depth, core_ref, x_ref, g_ref, before_ref, after_ref, slope_ref, pad_ref):
    length, width = x_ref.shape
    edge = before_ref.shape[0]
    order = order_rows(core_ref[0], width, depth)
    pad_ref[TOP - edge : TOP] = turn(before_ref[...], order)
    pad_ref[TOP : TOP + length] = turn(g_ref[...], order)
    pad_ref[TOP + length : TOP + length + edge] = turn(after_ref[...], order)
    normed = norm(x_ref[...])[2]
    slope_ref[...] = cumulative(normed) + normed * jnp.exp(-0.5 * normed * normed) * (
        0.3989422804014327
    )


def pair_body(mine_ref, got_ref, out_ref):
    blocks = mine_ref.shape[0]
    out_ref[:blocks] = (mine_ref[...] + got_ref[...].astype(F32)).astype(BF)
    for extra in range(blocks, out_ref.shape[0]):
        out_ref[extra] = jnp.zeros(out_ref.shape[1:], BF)


def plane_body(depth, plane_ref, row_ref, out_ref):
    total = plane_ref[0].astype(F32)
    for i in range(1, plane_ref.shape[0]):
        total = total + plane_ref[i].astype(F32)
    rows = row_ref[...].astype(F32)
    out_ref[0] = jnp.broadcast_to(rows[0:1], out_ref.shape[1:]).astype(BF)
    out_ref[1] = jnp.broadcast_to(rows[1:2], out_ref.shape[1:]).astype(BF)
    out_ref[2] = total[:depth].astype(BF)
    out_ref[3] = total[depth:].astype(BF)


def line_body(share, line_ref, out_ref):
    depth, width = line_ref.shape[1:]
    first = jnp.sum(line_ref[2].astype(F32), axis=0, keepdims=True) / share
    second = jnp.sum(line_ref[3].astype(F32), axis=0, keepdims=True) / share
    both = jnp.concatenate([first, second], axis=0)
    high = both.astype(BF).astype(F32)
    tail = jnp.concatenate([high, both - high, jnp.zeros((4, width), F32)], axis=0).astype(BF)
    for i in range(out_ref.shape[0]):
        out_ref[i, :depth] = line_ref[0]
        out_ref[i, depth : 2 * depth] = line_ref[1]
        out_ref[i, 2 * depth :] = tail


def conv_body(
    taps,
    depth,
    core_ref,
    x_ref,
    g_ref,
    slope_ref,
    act_pad_ref,
    cot_pad_ref,
    own_ref,
    far_ref,
    out_ref,
    grad_ref,
):
    length, width = x_ref.shape
    edge = (taps - 1) // 2
    pairs = width // (4 * depth)
    order = order_rows(core_ref[0], width, depth)
    weights = [
        jnp.concatenate(
            [
                ref[shift * pairs + i, : 2 * depth]
                for ref in (own_ref, far_ref)
                for i in range(pairs)
            ],
            axis=0,
        )
        for shift in range(taps)
    ]
    rows = length // 2
    for begin in range(0, length, rows):
        at = TOP - edge + begin
        total = jnp.zeros((rows, width), F32)
        carry = jnp.zeros((rows, width), F32)
        for shift in range(taps):
            window = act_pad_ref[at + shift : at + shift + rows].astype(BF)
            total = total + turn(window, weights[shift])
            back = at + 2 * edge - shift
            window = cot_pad_ref[back : back + rows].astype(BF)
            carry = carry + jnp.dot(window, weights[shift], preferred_element_type=F32)
        branch = jnp.dot(total.astype(BF), order, preferred_element_type=F32)
        inputs, scale, normed = norm(x_ref[begin : begin + rows])
        out_ref[begin : begin + rows] = (inputs + branch).astype(BF)
        normed_grad = carry * slope_ref[begin : begin + rows]
        project = jnp.mean(normed_grad * normed, axis=-1, keepdims=True)
        grad_ref[begin : begin + rows] = (
            g_ref[begin : begin + rows].astype(F32) + (normed_grad - normed * project) / scale
        ).astype(BF)


def local(section_input, kernel, cotangent):
    x = section_input[0]
    g = cotangent[0]
    length, width = x.shape
    held, taps, _ = kernel.shape
    edge = (taps - 1) // 2
    depth = lax.axis_size("z")
    groups = lax.axis_size(XY)
    count = lax.axis_size(SEQ)
    pairs = held // 2
    blocks = taps * pairs
    half = width // 2
    padded = length + 2 * TOP
    core = lax.axis_index("core").astype(jnp.int32).reshape(1)
    spot = lax.axis_index(XY)
    shape = jax.ShapeDtypeStruct
    swap = [(0, 1), (1, 0)]
    macs = length * width * width

    ends = jnp.concatenate([x[length - edge :], g[length - edge :]], axis=0)
    starts = jnp.concatenate([x[:edge], g[:edge]], axis=0)
    before = lax.ppermute(ends, SEQ, [(i, i + 1) for i in range(count - 1)])
    after = lax.ppermute(starts, SEQ, [(i + 1, i) for i in range(count - 1)])

    act, cot_t = call(
        functools.partial(act_body, depth),
        (shape((length, width), BF), shape((width, length), BF)),
        2 * macs,
        4 * length * width * 2,
        1,
        2,
    )(core, x, g)
    mine, other, act_pad = call(
        functools.partial(grad_body, taps),
        (
            shape((taps, half, width), F32),
            shape((taps, half, width), BF),
            shape((padded, width), F32),
        ),
        2 * taps * macs,
        8 * length * width * 2,
        0,
        4,
    )(act, cot_t, before[:edge], after[:edge])
    got = lax.ppermute(other, "core", swap)
    slope, cot_pad = call(
        functools.partial(slope_body, depth),
        (shape((length, width), F32), shape((padded, width), F32)),
        2 * macs,
        6 * length * width * 2,
        1,
        4,
    )(core, x, g, before[edge:], after[edge:])

    chip = call(
        pair_body,
        shape((groups, 2 * depth, width), BF),
        taps * half * width,
        taps * half * width * 8,
        0,
        2,
    )(mine.reshape(blocks, 2 * depth, width), got.reshape(blocks, 2 * depth, width))
    plane = lax.all_to_all(chip, XY, 0, 0)

    by_block = kernel.reshape(pairs, 2, taps, width).transpose(2, 0, 1, 3).reshape(blocks, 2, width)
    rows = lax.dynamic_index_in_dim(by_block, jnp.minimum(spot, blocks - 1), 0, keepdims=False)
    packed = call(
        functools.partial(plane_body, depth),
        shape((4, depth, width), BF),
        groups * 2 * depth * width,
        groups * 2 * depth * width * 2,
        0,
        2,
    )(plane, rows)
    line = lax.all_to_all(packed.transpose(1, 0, 2), "z", 0, 0).transpose(1, 0, 2)
    sent = call(
        functools.partial(line_body, float(groups * section_input.shape[0])),
        shape((groups, 2 * depth + 8, width), BF),
        4 * depth * width,
        groups * 2 * depth * width * 2,
        0,
        1,
    )(line)
    own = lax.all_to_all(sent, XY, 0, 0)
    far = lax.ppermute(own, "core", swap)

    sums = own[:blocks, 2 * depth : 2 * depth + 4].astype(F32)
    sums = (sums[:, :2] + sums[:, 2:]).reshape(taps, held, width)
    kernel_grad = sums.transpose(1, 0, 2)

    out, grad = call(
        functools.partial(conv_body, taps, depth),
        (shape((length, width), BF), shape((length, width), BF)),
        4 * taps * macs,
        12 * length * width * 2,
        1,
        7,
    )(core, x, g, slope, act_pad, cot_pad, own, far)
    return (out[None], grad[None], kernel_grad)


def solution(mesh):
    seq = mesh.shape["seq"]
    side = int(round(mesh.shape["dp"] ** 0.5))
    fine = Mesh(mesh.devices.reshape(side, side, seq // 2, 2), XY + SEQ)
    return jax.shard_map(
        local,
        mesh=fine,
        in_specs=(P(XY, SEQ, None), P(SEQ, None, None), P(XY, SEQ, None)),
        out_specs=(P(XY, SEQ, None), P(XY, SEQ, None), P(SEQ, None, None)),
        check_vma=False,
    )
```

```python
import functools

import jax
import jax.numpy as jnp
from jax import lax
from jax.experimental import pallas as pl
from jax.experimental.pallas import tpu as pltpu
from jax.sharding import Mesh, PartitionSpec as P

XY = ("x", "y")
SEQ = ("z", "core")
BF = jnp.bfloat16
F32 = jnp.float32
TOP = 8
VMEM_BYTES = 24 * 1024 * 1024
ALONE_BYTES = 63 * 1024 * 1024


def call(body, out_shape, flops, bytes_accessed, scalars=0, plain=0, scratch=(), far=0, vmem=VMEM_BYTES):
    specs = [pl.BlockSpec(memory_space=pltpu.SMEM)] * scalars
    specs += [pl.BlockSpec(memory_space=pltpu.VMEM)] * plain
    specs += [pl.BlockSpec(memory_space=pltpu.HBM)] * far
    outs = jax.tree.map(lambda _: pl.BlockSpec(memory_space=pltpu.VMEM), out_shape)
    return pl.pallas_call(
        body,
        out_shape=out_shape,
        in_specs=specs,
        out_specs=outs,
        scratch_shapes=list(scratch),
        compiler_params=pltpu.CompilerParams(vmem_limit_bytes=vmem),
        cost_estimate=pl.CostEstimate(
            flops=flops, bytes_accessed=bytes_accessed, transcendentals=0
        ),
    )


def norm(rows):
    inputs = rows.astype(F32)
    scale = jnp.sqrt(jnp.mean(inputs * inputs, axis=-1, keepdims=True) + 1e-05)
    return inputs, scale, inputs / scale


def cumulative(values):
    return 0.5 * (1.0 + lax.erf(values * 0.7071067811865476))


def gelu_rows(rows):
    normed = norm(rows)[2]
    return (normed * cumulative(normed)).astype(BF)


def order_rows(core, width, depth):
    half = width // 2
    held = width // (2 * depth)
    j = lax.broadcasted_iota(jnp.int32, (width, 1), 0)
    side = (j >= half).astype(jnp.int32)
    within = j - side * half
    pair = within // (2 * depth)
    member = (within // depth) % 2
    place = within % depth
    source = (place * 2 + (side + core) % 2) * held + 2 * pair + member
    o = lax.broadcasted_iota(jnp.int32, (width, width), 1)
    return jnp.where(o == source, 1.0, 0.0).astype(BF)


def turn(a, b):
    return lax.dot_general(a, b, (((1,), (1,)), ((), ())), preferred_element_type=F32)


def act_body(depth, core_ref, x_hbm, g_hbm, act_ref, cot_t_ref, x_ref, g_ref, sems):
    get_g = pltpu.make_async_copy(g_hbm, g_ref, sems.at[0])
    get_x = pltpu.make_async_copy(x_hbm, x_ref, sems.at[1])
    get_g.start()
    get_x.start()
    order = order_rows(core_ref[0], x_ref.shape[1], depth)
    get_g.wait()
    cot_t_ref[...] = turn(order, g_ref[...]).astype(BF)
    get_x.wait()
    act_ref[...] = gelu_rows(x_ref[...])


def fill_act(pad_ref, act, before_ref, after_ref, edge):
    length = act.shape[0]
    pad_ref[TOP - edge : TOP] = gelu_rows(before_ref[:edge]).astype(F32)
    pad_ref[TOP : TOP + length] = act.astype(F32)
    pad_ref[TOP + length : TOP + length + edge] = gelu_rows(after_ref[:edge]).astype(F32)


def grad_body(taps, pairs, act_ref, cot_t_ref, before_ref, after_ref, out_ref, pad_ref, *, side):
    length, width = act_ref.shape
    edge = (taps - 1) // 2
    half = width // 2
    rows = half // pairs
    fill_act(pad_ref, act_ref[...], before_ref, after_ref, edge)
    cot_t = cot_t_ref[side * half : (side + 1) * half]
    for shift in range(taps):
        begin = TOP - edge + shift
        window = pad_ref[begin : begin + length].astype(BF)
        part = jnp.dot(cot_t, window, preferred_element_type=F32).astype(out_ref.dtype)
        for i in range(pairs):
            out_ref[shift * pairs + i] = part[i * rows : (i + 1) * rows]


def pair_body(mine_ref, got_ref, out_ref):
    blocks = mine_ref.shape[0]
    out_ref[:blocks] = (mine_ref[...] + got_ref[...].astype(F32)).astype(BF)
    for extra in range(blocks, out_ref.shape[0]):
        out_ref[extra] = jnp.zeros(out_ref.shape[1:], BF)


def plane_body(depth, plane_ref, row_ref, out_ref):
    total = plane_ref[0].astype(F32)
    for i in range(1, plane_ref.shape[0]):
        total = total + plane_ref[i].astype(F32)
    rows = row_ref[...].astype(F32)
    out_ref[0] = jnp.broadcast_to(rows[0:1], out_ref.shape[1:]).astype(BF)
    out_ref[1] = jnp.broadcast_to(rows[1:2], out_ref.shape[1:]).astype(BF)
    out_ref[2] = total[:depth].astype(BF)
    out_ref[3] = total[depth:].astype(BF)


def line_body(share, line_ref, out_ref):
    depth, width = line_ref.shape[1:]
    first = jnp.sum(line_ref[2].astype(F32), axis=0, keepdims=True) / share
    second = jnp.sum(line_ref[3].astype(F32), axis=0, keepdims=True) / share
    both = jnp.concatenate([first, second], axis=0)
    high = both.astype(BF).astype(F32)
    tail = jnp.concatenate([high, both - high, jnp.zeros((4, width), F32)], axis=0).astype(BF)
    for i in range(out_ref.shape[0]):
        out_ref[i, :depth] = line_ref[0]
        out_ref[i, depth : 2 * depth] = line_ref[1]
        out_ref[i, 2 * depth :] = tail


def weight(ref, shift, pairs, rows):
    return jnp.concatenate([ref[shift * pairs + i, :rows] for i in range(pairs)], axis=0)


def near_body(
    taps,
    depth,
    core_ref,
    x_ref,
    g_ref,
    before_ref,
    after_ref,
    own_ref,
    near_ref,
    act_ref,
    cot_ref,
    kernel_grad_ref,
    pad_ref,
):
    length, width = x_ref.shape
    edge = (taps - 1) // 2
    pairs = width // (4 * depth)
    order = order_rows(core_ref[0], width, depth)
    fill_act(pad_ref, gelu_rows(x_ref[...]), before_ref, after_ref, edge)
    act_ref[...] = pad_ref[...].astype(BF)
    total = jnp.zeros((length, width // 2), F32)
    for shift in range(taps):
        begin = TOP - edge + shift
        window = pad_ref[begin : begin + length].astype(BF)
        total = total + turn(window, weight(own_ref, shift, pairs, 2 * depth))
    near_ref[...] = total.astype(BF)
    cot_ref[TOP : TOP + length] = turn(g_ref[...], order).astype(BF)
    zeros = jnp.zeros((TOP - edge, width), F32)
    first = turn(before_ref[edge:], order)
    last = turn(after_ref[edge:], order)
    cot_ref[:TOP] = jnp.concatenate([zeros, first], axis=0).astype(BF)
    cot_ref[TOP + length :] = jnp.concatenate([last, zeros], axis=0).astype(BF)
    for shift in range(taps):
        for i in range(pairs):
            value = own_ref[shift * pairs + i, 2 * depth :].astype(F32)
            kernel_grad_ref[shift, 2 * i : 2 * i + 2] = value[:2] + value[2:4]


def far_body(
    taps,
    depth,
    core_ref,
    x_ref,
    g_ref,
    near_ref,
    act_ref,
    cot_ref,
    own_ref,
    far_ref,
    out_ref,
    grad_ref,
    act_pad_ref,
    cot_pad_ref,
):
    length, width = x_ref.shape
    edge = (taps - 1) // 2
    pairs = width // (4 * depth)
    act_pad_ref[...] = act_ref[...].astype(F32)
    cot_pad_ref[...] = cot_ref[...].astype(F32)
    order = order_rows(core_ref[0], width, depth)
    own = [weight(own_ref, shift, pairs, 2 * depth) for shift in range(taps)]
    far = [weight(far_ref, shift, pairs, 2 * depth) for shift in range(taps)]
    rows = length // 2
    for begin in range(0, length, rows):
        at = TOP - edge + begin
        total = jnp.zeros((rows, width // 2), F32)
        carry = jnp.zeros((rows, width), F32)
        for shift in range(taps):
            back = at + 2 * edge - shift
            window = cot_pad_ref[back : back + rows].astype(BF)
            both = jnp.concatenate([own[shift], far[shift]], axis=0)
            carry = carry + jnp.dot(window, both, preferred_element_type=F32)
            window = act_pad_ref[at + shift : at + shift + rows].astype(BF)
            total = total + turn(window, far[shift])
        grouped = jnp.concatenate([near_ref[begin : begin + rows], total.astype(BF)], axis=1)
        branch = jnp.dot(grouped, order, preferred_element_type=F32)
        inputs, scale, normed = norm(x_ref[begin : begin + rows])
        out_ref[begin : begin + rows] = (inputs + branch).astype(BF)
        slope = cumulative(normed) + normed * jnp.exp(-0.5 * normed * normed) * (
            0.3989422804014327
        )
        normed_grad = carry * slope
        project = jnp.mean(normed_grad * normed, axis=-1, keepdims=True)
        grad_ref[begin : begin + rows] = (
            g_ref[begin : begin + rows].astype(F32) + (normed_grad - normed * project) / scale
        ).astype(BF)


def local(section_input, kernel, cotangent):
    x = section_input[0]
    g = cotangent[0]
    length, width = x.shape
    held, taps, _ = kernel.shape
    edge = (taps - 1) // 2
    depth = lax.axis_size("z")
    groups = lax.axis_size(XY)
    count = lax.axis_size(SEQ)
    pairs = held // 2
    blocks = taps * pairs
    half = width // 2
    padded = length + 2 * TOP
    core = lax.axis_index("core").astype(jnp.int32).reshape(1)
    spot = lax.axis_index(XY)
    shape = jax.ShapeDtypeStruct
    swap = [(0, 1), (1, 0)]
    macs = length * width * width

    ends = jnp.concatenate([x[length - edge :], g[length - edge :]], axis=0)
    starts = jnp.concatenate([x[:edge], g[:edge]], axis=0)
    before = lax.ppermute(ends, SEQ, [(i, i + 1) for i in range(count - 1)])
    after = lax.ppermute(starts, SEQ, [(i + 1, i) for i in range(count - 1)])

    whole = pltpu.VMEM((length, width), BF)
    pad = pltpu.VMEM((padded, width), F32)
    act, cot_t = call(
        functools.partial(act_body, depth),
        (shape((length, width), BF), shape((width, length), BF)),
        2 * macs,
        4 * length * width * 2,
        1,
        0,
        [whole, whole, pltpu.SemaphoreType.DMA((2,))],
        2,
        ALONE_BYTES,
    )(core, x, g)
    sides = [
        call(
            functools.partial(grad_body, taps, pairs, side=side),
            shape((blocks, 2 * depth, width), kind),
            taps * macs,
            8 * length * width * 2,
            0,
            4,
            [pad],
        )
        for side, kind in ((0, F32), (1, BF))
    ]
    other = sides[1](act, cot_t, before, after)
    got = lax.ppermute(other, "core", swap)
    mine = sides[0](act, cot_t, before, after)
    chip = call(
        pair_body,
        shape((groups, 2 * depth, width), BF),
        taps * half * width,
        taps * half * width * 8,
        0,
        2,
    )(mine, got)
    plane = lax.all_to_all(chip, XY, 0, 0)

    by_block = kernel.reshape(pairs, 2, taps, width).transpose(2, 0, 1, 3).reshape(blocks, 2, width)
    rows = lax.dynamic_index_in_dim(by_block, jnp.minimum(spot, blocks - 1), 0, keepdims=False)
    packed = call(
        functools.partial(plane_body, depth),
        shape((4, depth, width), BF),
        groups * 2 * depth * width,
        groups * 2 * depth * width * 2,
        0,
        2,
    )(plane, rows)
    line = lax.all_to_all(packed.transpose(1, 0, 2), "z", 0, 0).transpose(1, 0, 2)
    sent = call(
        functools.partial(line_body, float(groups * section_input.shape[0])),
        shape((groups, 2 * depth + 8, width), BF),
        4 * depth * width,
        groups * 2 * depth * width * 2,
        0,
        1,
    )(line)
    own = lax.all_to_all(sent, XY, 0, 0)
    far = lax.ppermute(own, "core", swap)

    near, act_rows, cot_rows, kernel_grad = call(
        functools.partial(near_body, taps, depth),
        (
            shape((length, half), BF),
            shape((padded, width), BF),
            shape((padded, width), BF),
            shape((taps, held, width), F32),
        ),
        2 * taps * macs,
        8 * length * width * 2,
        1,
        5,
        [pad],
    )(core, x, g, before, after, own)
    out, grad = call(
        functools.partial(far_body, taps, depth),
        (shape((length, width), BF), shape((length, width), BF)),
        4 * taps * macs,
        12 * length * width * 2,
        1,
        7,
        [pad, pad],
    )(core, x, g, near, act_rows, cot_rows, own, far)
    return (out[None], grad[None], kernel_grad.transpose(1, 0, 2))


def solution(mesh):
    seq = mesh.shape["seq"]
    side = int(round(mesh.shape["dp"] ** 0.5))
    fine = Mesh(mesh.devices.reshape(side, side, seq // 2, 2), XY + SEQ)
    return jax.shard_map(
        local,
        mesh=fine,
        in_specs=(P(XY, SEQ, None), P(SEQ, None, None), P(XY, SEQ, None)),
        out_specs=(P(XY, SEQ, None), P(XY, SEQ, None), P(SEQ, None, None)),
        check_vma=False,
    )
```

```python
import functools

import jax
import jax.numpy as jnp
from jax import lax
from jax.experimental import pallas as pl
from jax.experimental.pallas import tpu as pltpu
from jax.sharding import Mesh, PartitionSpec as P

XY = ("x", "y")
SEQ = ("z", "core")
BF = jnp.bfloat16
F32 = jnp.float32
TOP = 8
VMEM_BYTES = 24 * 1024 * 1024


def call(body, out_shape, flops, bytes_accessed, scalars=0, plain=0, scratch=(), far=0):
    specs = [pl.BlockSpec(memory_space=pltpu.SMEM)] * scalars
    specs += [pl.BlockSpec(memory_space=pltpu.VMEM)] * plain
    specs += [pl.BlockSpec(memory_space=pl.ANY)] * far
    outs = jax.tree.map(lambda _: pl.BlockSpec(memory_space=pltpu.VMEM), out_shape)
    return pl.pallas_call(
        body,
        out_shape=out_shape,
        in_specs=specs,
        out_specs=outs,
        scratch_shapes=list(scratch),
        compiler_params=pltpu.CompilerParams(vmem_limit_bytes=VMEM_BYTES),
        cost_estimate=pl.CostEstimate(
            flops=flops, bytes_accessed=bytes_accessed, transcendentals=0
        ),
    )


def norm(rows):
    inputs = rows.astype(F32)
    scale = jnp.sqrt(jnp.mean(inputs * inputs, axis=-1, keepdims=True) + 1e-05)
    return inputs, scale, inputs / scale


def cumulative(values):
    return 0.5 * (1.0 + lax.erf(values * 0.7071067811865476))


def gelu_rows(rows):
    normed = norm(rows)[2]
    return (normed * cumulative(normed)).astype(BF)


def order_rows(core, width, depth):
    half = width // 2
    held = width // (2 * depth)
    j = lax.broadcasted_iota(jnp.int32, (width, 1), 0)
    side = (j >= half).astype(jnp.int32)
    within = j - side * half
    pair = within // (2 * depth)
    member = (within // depth) % 2
    place = within % depth
    source = (place * 2 + (side + core) % 2) * held + 2 * pair + member
    o = lax.broadcasted_iota(jnp.int32, (width, width), 1)
    return jnp.where(o == source, 1.0, 0.0).astype(BF)


def turn(a, b):
    return lax.dot_general(a, b, (((1,), (1,)), ((), ())), preferred_element_type=F32)


def act_body(depth, core_ref, x_ref, g_ref, act_ref, cot_t_ref):
    order = order_rows(core_ref[0], x_ref.shape[1], depth)
    cot_t_ref[...] = turn(order, g_ref[...]).astype(BF)
    act_ref[...] = gelu_rows(x_ref[...])


def fill_act(pad_ref, act, before_ref, after_ref, edge):
    length = act.shape[0]
    pad_ref[TOP - edge : TOP] = gelu_rows(before_ref[:edge]).astype(F32)
    pad_ref[TOP : TOP + length] = act.astype(F32)
    pad_ref[TOP + length : TOP + length + edge] = gelu_rows(after_ref[:edge]).astype(F32)


def grad_body(taps, pairs, act_ref, cot_t_ref, before_ref, after_ref, out_ref, pad_ref, *, side):
    length, width = act_ref.shape
    edge = (taps - 1) // 2
    half = width // 2
    rows = half // pairs
    fill_act(pad_ref, act_ref[...], before_ref, after_ref, edge)
    cot_t = cot_t_ref[side * half : (side + 1) * half]
    for shift in range(taps):
        begin = TOP - edge + shift
        window = pad_ref[begin : begin + length].astype(BF)
        part = jnp.dot(cot_t, window, preferred_element_type=F32).astype(out_ref.dtype)
        for i in range(pairs):
            out_ref[shift * pairs + i] = part[i * rows : (i + 1) * rows]


def pair_body(mine_ref, got_ref, out_ref):
    blocks = mine_ref.shape[0]
    out_ref[:blocks] = (mine_ref[...] + got_ref[...].astype(F32)).astype(BF)
    for extra in range(blocks, out_ref.shape[0]):
        out_ref[extra] = jnp.zeros(out_ref.shape[1:], BF)


def plane_body(depth, plane_ref, row_ref, out_ref):
    total = plane_ref[0].astype(F32)
    for i in range(1, plane_ref.shape[0]):
        total = total + plane_ref[i].astype(F32)
    rows = row_ref[...].astype(F32)
    out_ref[0] = jnp.broadcast_to(rows[0:1], out_ref.shape[1:]).astype(BF)
    out_ref[1] = jnp.broadcast_to(rows[1:2], out_ref.shape[1:]).astype(BF)
    out_ref[2] = total[:depth].astype(BF)
    out_ref[3] = total[depth:].astype(BF)


def line_body(share, line_ref, after_ref, out_ref):
    del after_ref
    depth, width = line_ref.shape[1:]
    first = jnp.sum(line_ref[2].astype(F32), axis=0, keepdims=True) / share
    second = jnp.sum(line_ref[3].astype(F32), axis=0, keepdims=True) / share
    both = jnp.concatenate([first, second], axis=0)
    high = both.astype(BF).astype(F32)
    tail = jnp.concatenate([high, both - high, jnp.zeros((4, width), F32)], axis=0).astype(BF)
    for i in range(out_ref.shape[0]):
        out_ref[i, :depth] = line_ref[0]
        out_ref[i, depth : 2 * depth] = line_ref[1]
        out_ref[i, 2 * depth :] = tail


def weight(ref, shift, pairs, rows):
    return jnp.concatenate([ref[shift * pairs + i, :rows] for i in range(pairs)], axis=0)


def prep_body(
    depth,
    core_ref,
    x_ref,
    g_ref,
    before_ref,
    after_ref,
    packed_ref,
    act_ref,
    cot_ref,
    slope_ref,
):
    del packed_ref
    length, width = x_ref.shape
    edge = before_ref.shape[0] // 2
    order = order_rows(core_ref[0], width, depth)
    zeros = jnp.zeros((TOP - edge, width), F32)
    normed = norm(x_ref[...])[2]
    share = cumulative(normed)
    act_ref[TOP : TOP + length] = (normed * share).astype(BF)
    first = gelu_rows(before_ref[:edge]).astype(F32)
    last = gelu_rows(after_ref[:edge]).astype(F32)
    act_ref[:TOP] = jnp.concatenate([zeros, first], axis=0).astype(BF)
    act_ref[TOP + length :] = jnp.concatenate([last, zeros], axis=0).astype(BF)
    cot_ref[TOP : TOP + length] = turn(g_ref[...], order).astype(BF)
    first = turn(before_ref[edge:], order)
    last = turn(after_ref[edge:], order)
    cot_ref[:TOP] = jnp.concatenate([zeros, first], axis=0).astype(BF)
    cot_ref[TOP + length :] = jnp.concatenate([last, zeros], axis=0).astype(BF)
    slope_ref[...] = share + normed * jnp.exp(-0.5 * normed * normed) * 0.3989422804014327


def half_convs(weights, act_pad_ref, cot_pad_ref, side, begin, rows):
    taps = len(weights)
    half, width = weights[0].shape
    edge = (taps - 1) // 2
    at = TOP - edge + begin
    total = jnp.zeros((rows, half), F32)
    carry = jnp.zeros((rows, width), F32)
    for shift in range(taps):
        window = act_pad_ref[at + shift : at + shift + rows].astype(BF)
        total = total + turn(window, weights[shift])
        back = at + 2 * edge - shift
        window = cot_pad_ref[back : back + rows].astype(BF)[:, side * half : (side + 1) * half]
        carry = carry + jnp.dot(window, weights[shift], preferred_element_type=F32)
    return total.astype(BF), carry


def near_body(
    taps,
    depth,
    act_ref,
    cot_ref,
    own_ref,
    near_ref,
    carry_ref,
    kernel_grad_ref,
    act_pad_ref,
    cot_pad_ref,
):
    length, half = near_ref.shape
    pairs = half // (2 * depth)
    act_pad_ref[...] = act_ref[...].astype(F32)
    cot_pad_ref[...] = cot_ref[...].astype(F32)
    own = [weight(own_ref, shift, pairs, 2 * depth) for shift in range(taps)]
    rows = length // 2
    for begin in range(0, length, rows):
        near_ref[begin : begin + rows], carry_ref[begin : begin + rows] = half_convs(
            own, act_pad_ref, cot_pad_ref, 0, begin, rows
        )
    for shift in range(taps):
        for i in range(pairs):
            value = own_ref[shift * pairs + i, 2 * depth :].astype(F32)
            kernel_grad_ref[shift, 2 * i : 2 * i + 2] = value[:2] + value[2:4]


def far_body(
    taps,
    depth,
    core_ref,
    x_ref,
    g_ref,
    slope_ref,
    near_ref,
    carry_ref,
    act_ref,
    cot_ref,
    far_ref,
    out_ref,
    grad_ref,
    act_pad_ref,
    cot_pad_ref,
):
    length, width = x_ref.shape
    pairs = width // (4 * depth)
    act_pad_ref[...] = act_ref[...].astype(F32)
    cot_pad_ref[...] = cot_ref[...].astype(F32)
    order = order_rows(core_ref[0], width, depth)
    far = [weight(far_ref, shift, pairs, 2 * depth) for shift in range(taps)]
    rows = length // 2
    for begin in range(0, length, rows):
        total, carry = half_convs(far, act_pad_ref, cot_pad_ref, 1, begin, rows)
        carry = carry + carry_ref[begin : begin + rows]
        grouped = jnp.concatenate([near_ref[begin : begin + rows], total], axis=1)
        branch = jnp.dot(grouped, order, preferred_element_type=F32)
        inputs, scale, normed = norm(x_ref[begin : begin + rows])
        out_ref[begin : begin + rows] = (inputs + branch).astype(BF)
        normed_grad = carry * slope_ref[begin : begin + rows]
        project = jnp.mean(normed_grad * normed, axis=-1, keepdims=True)
        grad_ref[begin : begin + rows] = (
            g_ref[begin : begin + rows].astype(F32) + (normed_grad - normed * project) / scale
        ).astype(BF)


def local(section_input, kernel, cotangent):
    x = section_input[0]
    g = cotangent[0]
    length, width = x.shape
    held, taps, _ = kernel.shape
    edge = (taps - 1) // 2
    depth = lax.axis_size("z")
    groups = lax.axis_size(XY)
    count = lax.axis_size(SEQ)
    pairs = held // 2
    blocks = taps * pairs
    half = width // 2
    padded = length + 2 * TOP
    core = lax.axis_index("core").astype(jnp.int32).reshape(1)
    spot = lax.axis_index(XY)
    shape = jax.ShapeDtypeStruct
    swap = [(0, 1), (1, 0)]
    macs = length * width * width

    ends = jnp.concatenate([x[length - edge :], g[length - edge :]], axis=0)
    starts = jnp.concatenate([x[:edge], g[:edge]], axis=0)
    before = lax.ppermute(ends, SEQ, [(i, i + 1) for i in range(count - 1)])
    after = lax.ppermute(starts, SEQ, [(i + 1, i) for i in range(count - 1)])

    pad = pltpu.VMEM((padded, width), F32)
    act, cot_t = call(
        functools.partial(act_body, depth),
        (shape((length, width), BF), shape((width, length), BF)),
        2 * macs,
        4 * length * width * 2,
        1,
        2,
    )(core, x, g)
    sides = [
        call(
            functools.partial(grad_body, taps, pairs, side=side),
            shape((blocks, 2 * depth, width), kind),
            taps * macs,
            8 * length * width * 2,
            0,
            4,
            [pad],
        )
        for side, kind in ((0, F32), (1, BF))
    ]
    other = sides[1](act, cot_t, before, after)
    got = lax.ppermute(other, "core", swap)
    mine = sides[0](act, cot_t, before, after)
    chip = call(
        pair_body,
        shape((groups, 2 * depth, width), BF),
        taps * half * width,
        taps * half * width * 8,
        0,
        2,
    )(mine, got)
    plane = lax.all_to_all(chip, XY, 0, 0)

    by_block = kernel.reshape(pairs, 2, taps, width).transpose(2, 0, 1, 3).reshape(blocks, 2, width)
    rows = lax.dynamic_index_in_dim(by_block, jnp.minimum(spot, blocks - 1), 0, keepdims=False)
    packed = call(
        functools.partial(plane_body, depth),
        shape((4, depth, width), BF),
        groups * 2 * depth * width,
        groups * 2 * depth * width * 2,
        0,
        2,
    )(plane, rows)
    act_rows, cot_rows, slope = call(
        functools.partial(prep_body, depth),
        (shape((padded, width), BF), shape((padded, width), BF), shape((length, width), F32)),
        2 * macs,
        8 * length * width * 2,
        1,
        4,
        far=1,
    )(core, x, g, before, after, packed)
    line = lax.all_to_all(packed.transpose(1, 0, 2), "z", 0, 0).transpose(1, 0, 2)
    sent = call(
        functools.partial(line_body, float(groups * section_input.shape[0])),
        shape((groups, 2 * depth + 8, width), BF),
        4 * depth * width,
        groups * 2 * depth * width * 2,
        0,
        1,
        far=1,
    )(line, act_rows)
    own = lax.all_to_all(sent, XY, 0, 0)
    far = lax.ppermute(own, "core", swap)

    near, carry, kernel_grad = call(
        functools.partial(near_body, taps, depth),
        (
            shape((length, half), BF),
            shape((length, width), F32),
            shape((taps, held, width), F32),
        ),
        2 * taps * macs,
        8 * length * width * 2,
        0,
        3,
        [pad, pad],
    )(act_rows, cot_rows, own)
    out, grad = call(
        functools.partial(far_body, taps, depth),
        (shape((length, width), BF), shape((length, width), BF)),
        2 * taps * macs,
        12 * length * width * 2,
        1,
        8,
        [pad, pad],
    )(core, x, g, slope, near, carry, act_rows, cot_rows, far)
    return (out[None], grad[None], kernel_grad.transpose(1, 0, 2))


def solution(mesh):
    seq = mesh.shape["seq"]
    side = int(round(mesh.shape["dp"] ** 0.5))
    fine = Mesh(mesh.devices.reshape(side, side, seq // 2, 2), XY + SEQ)
    return jax.shard_map(
        local,
        mesh=fine,
        in_specs=(P(XY, SEQ, None), P(SEQ, None, None), P(XY, SEQ, None)),
        out_specs=(P(XY, SEQ, None), P(XY, SEQ, None), P(SEQ, None, None)),
        check_vma=False,
    )
```

```python
import functools

import jax
import jax.numpy as jnp
from jax import lax
from jax.experimental import pallas as pl
from jax.experimental.pallas import tpu as pltpu
from jax.sharding import Mesh, PartitionSpec as P

XY = ("x", "y")
SEQ = ("z", "core")
BF = jnp.bfloat16
F32 = jnp.float32
TOP = 8
VMEM_BYTES = 24 * 1024 * 1024


def call(body, out_shape, flops, bytes_accessed, scalars=0, plain=0, scratch=(), far=0):
    specs = [pl.BlockSpec(memory_space=pltpu.SMEM)] * scalars
    specs += [pl.BlockSpec(memory_space=pltpu.VMEM)] * plain
    specs += [pl.BlockSpec(memory_space=pl.ANY)] * far
    outs = jax.tree.map(lambda _: pl.BlockSpec(memory_space=pltpu.VMEM), out_shape)
    return pl.pallas_call(
        body,
        out_shape=out_shape,
        in_specs=specs,
        out_specs=outs,
        scratch_shapes=list(scratch),
        compiler_params=pltpu.CompilerParams(vmem_limit_bytes=VMEM_BYTES),
        cost_estimate=pl.CostEstimate(
            flops=flops, bytes_accessed=bytes_accessed, transcendentals=0
        ),
    )


def norm(rows):
    inputs = rows.astype(F32)
    scale = jnp.sqrt(jnp.mean(inputs * inputs, axis=-1, keepdims=True) + 1e-05)
    return inputs, scale, inputs / scale


def cumulative(values):
    return 0.5 * (1.0 + lax.erf(values * 0.7071067811865476))


def gelu_rows(rows):
    normed = norm(rows)[2]
    return (normed * cumulative(normed)).astype(BF)


def order_rows(core, width, depth):
    half = width // 2
    held = width // (2 * depth)
    j = lax.broadcasted_iota(jnp.int32, (width, 1), 0)
    side = (j >= half).astype(jnp.int32)
    within = j - side * half
    pair = within // (2 * depth)
    member = (within // depth) % 2
    place = within % depth
    source = (place * 2 + (side + core) % 2) * held + 2 * pair + member
    o = lax.broadcasted_iota(jnp.int32, (width, width), 1)
    return jnp.where(o == source, 1.0, 0.0).astype(BF)


def turn(a, b):
    return lax.dot_general(a, b, (((1,), (1,)), ((), ())), preferred_element_type=F32)


def local_grad(act_ref, cot_t, out_ref, pad_ref, taps, pairs):
    length, width = act_ref.shape
    edge = (taps - 1) // 2
    rows = cot_t.shape[0] // pairs
    pad_ref[:TOP] = jnp.zeros((TOP, width), F32)
    pad_ref[TOP : TOP + length] = act_ref[...].astype(F32)
    pad_ref[TOP + length :] = jnp.zeros((TOP, width), F32)
    for shift in range(taps):
        begin = TOP - edge + shift
        window = pad_ref[begin : begin + length].astype(BF)
        part = jnp.dot(cot_t, window, preferred_element_type=F32).astype(out_ref.dtype)
        for i in range(pairs):
            out_ref[shift * pairs + i] = part[i * rows : (i + 1) * rows]


def other_body(
    taps,
    pairs,
    depth,
    core_ref,
    x_ref,
    g_ref,
    out_ref,
    act_ref,
    cot_t_ref,
    starts_ref,
    ends_ref,
    pad_ref,
):
    length, width = x_ref.shape
    half = width // 2
    edge = (taps - 1) // 2
    first = [ref[:TOP].astype(F32)[:edge] for ref in (x_ref, g_ref)]
    last = [ref[length - TOP :].astype(F32)[TOP - edge :] for ref in (x_ref, g_ref)]
    starts_ref[...] = jnp.concatenate(first, axis=0).astype(BF)
    ends_ref[...] = jnp.concatenate(last, axis=0).astype(BF)
    order = order_rows(core_ref[0], width, depth)
    cot_t_ref[...] = turn(order, g_ref[...]).astype(BF)
    act_ref[...] = gelu_rows(x_ref[...])
    local_grad(act_ref, cot_t_ref[half:], out_ref, pad_ref, taps, pairs)


def mine_body(taps, pairs, act_ref, cot_t_ref, out_ref, pad_ref):
    half = cot_t_ref.shape[0] // 2
    local_grad(act_ref, cot_t_ref[:half], out_ref, pad_ref, taps, pairs)


def pair_body(
    taps,
    depth,
    core_ref,
    mine_ref,
    got_ref,
    before_ref,
    starts_ref,
    ends_ref,
    after_ref,
    out_ref,
):
    blocks, rows, width = mine_ref.shape
    edge = (taps - 1) // 2
    pairs = blocks // taps
    half = width // 2
    parts = [ref[...].astype(F32) for ref in (before_ref, starts_ref, ends_ref, after_ref)]
    act = gelu_rows(jnp.concatenate([p[:edge] for p in parts], axis=0)).astype(F32)
    cot = jnp.concatenate([p[edge:] for p in parts], axis=0).astype(BF)
    order = order_rows(core_ref[0], width, depth)
    cot_t = turn(order, cot)[:half].astype(BF)
    side = 2 * edge
    for shift in range(taps):
        offset = shift - edge
        window = []
        for i in range(2 * side):
            at = i % side
            to = at + offset
            crosses = 0 <= to < side and (at < edge) != (to < edge)
            row = i + offset
            window.append(act[row : row + 1] if crosses else jnp.zeros((1, width), F32))
        extra = jnp.dot(
            cot_t, jnp.concatenate(window, axis=0).astype(BF), preferred_element_type=F32
        )
        for i in range(pairs):
            j = shift * pairs + i
            out_ref[j] = (
                mine_ref[j] + got_ref[j].astype(F32) + extra[i * rows : (i + 1) * rows]
            ).astype(BF)
    for j in range(blocks, out_ref.shape[0]):
        out_ref[j] = jnp.zeros((rows, width), BF)


def plane_body(depth, plane_ref, row_ref, out_ref):
    total = plane_ref[0].astype(F32)
    for i in range(1, plane_ref.shape[0]):
        total = total + plane_ref[i].astype(F32)
    rows = row_ref[...].astype(F32)
    out_ref[0] = jnp.broadcast_to(rows[0:1], out_ref.shape[1:]).astype(BF)
    out_ref[1] = jnp.broadcast_to(rows[1:2], out_ref.shape[1:]).astype(BF)
    out_ref[2] = total[:depth].astype(BF)
    out_ref[3] = total[depth:].astype(BF)


def line_body(share, line_ref, after_ref, out_ref):
    del after_ref
    depth, width = line_ref.shape[1:]
    first = jnp.sum(line_ref[2].astype(F32), axis=0, keepdims=True) / share
    second = jnp.sum(line_ref[3].astype(F32), axis=0, keepdims=True) / share
    both = jnp.concatenate([first, second], axis=0)
    high = both.astype(BF).astype(F32)
    tail = jnp.concatenate([high, both - high, jnp.zeros((4, width), F32)], axis=0).astype(BF)
    for i in range(out_ref.shape[0]):
        out_ref[i, :depth] = line_ref[0]
        out_ref[i, depth : 2 * depth] = line_ref[1]
        out_ref[i, 2 * depth :] = tail


def weight(ref, shift, pairs, rows):
    return jnp.concatenate([ref[shift * pairs + i, :rows] for i in range(pairs)], axis=0)


def prep_body(
    depth,
    core_ref,
    x_ref,
    g_ref,
    before_ref,
    after_ref,
    packed_ref,
    act_ref,
    cot_ref,
    slope_ref,
):
    del packed_ref
    length, width = x_ref.shape
    edge = before_ref.shape[0] // 2
    order = order_rows(core_ref[0], width, depth)
    zeros = jnp.zeros((TOP - edge, width), F32)
    normed = norm(x_ref[...])[2]
    share = cumulative(normed)
    act_ref[TOP : TOP + length] = (normed * share).astype(BF)
    first = gelu_rows(before_ref[:edge]).astype(F32)
    last = gelu_rows(after_ref[:edge]).astype(F32)
    act_ref[:TOP] = jnp.concatenate([zeros, first], axis=0).astype(BF)
    act_ref[TOP + length :] = jnp.concatenate([last, zeros], axis=0).astype(BF)
    cot_ref[TOP : TOP + length] = turn(g_ref[...], order).astype(BF)
    first = turn(before_ref[edge:], order)
    last = turn(after_ref[edge:], order)
    cot_ref[:TOP] = jnp.concatenate([zeros, first], axis=0).astype(BF)
    cot_ref[TOP + length :] = jnp.concatenate([last, zeros], axis=0).astype(BF)
    slope_ref[...] = share + normed * jnp.exp(-0.5 * normed * normed) * 0.3989422804014327


def half_convs(weights, act_pad_ref, cot_pad_ref, side, begin, rows):
    taps = len(weights)
    half, width = weights[0].shape
    edge = (taps - 1) // 2
    at = TOP - edge + begin
    windows = [act_pad_ref[at + shift : at + shift + rows].astype(BF) for shift in range(taps)]
    total = turn(jnp.concatenate(windows, axis=1), jnp.concatenate(weights, axis=1))
    carry = jnp.zeros((rows, width), F32)
    for shift in range(taps):
        back = at + 2 * edge - shift
        window = cot_pad_ref[back : back + rows].astype(BF)[:, side * half : (side + 1) * half]
        carry = carry + jnp.dot(window, weights[shift], preferred_element_type=F32)
    return total.astype(BF), carry


def near_body(
    taps,
    depth,
    act_ref,
    cot_ref,
    own_ref,
    near_ref,
    carry_ref,
    kernel_grad_ref,
    act_pad_ref,
    cot_pad_ref,
):
    length, half = near_ref.shape
    pairs = half // (2 * depth)
    act_pad_ref[...] = act_ref[...].astype(F32)
    cot_pad_ref[...] = cot_ref[...].astype(F32)
    own = [weight(own_ref, shift, pairs, 2 * depth) for shift in range(taps)]
    rows = length // 2
    for begin in range(0, length, rows):
        near_ref[begin : begin + rows], carry_ref[begin : begin + rows] = half_convs(
            own, act_pad_ref, cot_pad_ref, 0, begin, rows
        )
    for shift in range(taps):
        for i in range(pairs):
            value = own_ref[shift * pairs + i, 2 * depth :].astype(F32)
            kernel_grad_ref[shift, 2 * i : 2 * i + 2] = value[:2] + value[2:4]


def far_body(
    taps,
    depth,
    core_ref,
    x_ref,
    g_ref,
    slope_ref,
    near_ref,
    carry_ref,
    act_ref,
    cot_ref,
    far_ref,
    out_ref,
    grad_ref,
    act_pad_ref,
    cot_pad_ref,
):
    length, width = x_ref.shape
    pairs = width // (4 * depth)
    act_pad_ref[...] = act_ref[...].astype(F32)
    cot_pad_ref[...] = cot_ref[...].astype(F32)
    order = order_rows(core_ref[0], width, depth)
    far = [weight(far_ref, shift, pairs, 2 * depth) for shift in range(taps)]
    rows = length // 2
    for begin in range(0, length, rows):
        total, carry = half_convs(far, act_pad_ref, cot_pad_ref, 1, begin, rows)
        carry = carry + carry_ref[begin : begin + rows]
        grouped = jnp.concatenate([near_ref[begin : begin + rows], total], axis=1)
        branch = jnp.dot(grouped, order, preferred_element_type=F32)
        inputs, scale, normed = norm(x_ref[begin : begin + rows])
        out_ref[begin : begin + rows] = (inputs + branch).astype(BF)
        normed_grad = carry * slope_ref[begin : begin + rows]
        project = jnp.mean(normed_grad * normed, axis=-1, keepdims=True)
        grad_ref[begin : begin + rows] = (
            g_ref[begin : begin + rows].astype(F32) + (normed_grad - normed * project) / scale
        ).astype(BF)


def local(section_input, kernel, cotangent):
    x = section_input[0]
    g = cotangent[0]
    length, width = x.shape
    held, taps, _ = kernel.shape
    edge = (taps - 1) // 2
    depth = lax.axis_size("z")
    groups = lax.axis_size(XY)
    count = lax.axis_size(SEQ)
    pairs = held // 2
    blocks = taps * pairs
    half = width // 2
    padded = length + 2 * TOP
    core = lax.axis_index("core").astype(jnp.int32).reshape(1)
    spot = lax.axis_index(XY)
    shape = jax.ShapeDtypeStruct
    swap = [(0, 1), (1, 0)]
    macs = length * width * width

    pad = pltpu.VMEM((padded, width), F32)
    block = (blocks, 2 * depth, width)
    rim = shape((2 * edge, width), BF)
    other, act, cot_t, starts, ends = call(
        functools.partial(other_body, taps, pairs, depth),
        (shape(block, BF), shape((length, width), BF), shape((width, length), BF), rim, rim),
        2 * macs + taps * macs,
        8 * length * width * 2,
        1,
        2,
        [pad],
    )(core, x, g)
    got = lax.ppermute(other, "core", swap)
    before = lax.ppermute(ends, SEQ, [(i, i + 1) for i in range(count - 1)])
    after = lax.ppermute(starts, SEQ, [(i + 1, i) for i in range(count - 1)])
    mine = call(
        functools.partial(mine_body, taps, pairs),
        shape(block, F32),
        taps * macs,
        8 * length * width * 2,
        0,
        2,
        [pad],
    )(act, cot_t)
    chip = call(
        functools.partial(pair_body, taps, depth),
        shape((groups, 2 * depth, width), BF),
        taps * half * width,
        taps * half * width * 8,
        1,
        6,
    )(core, mine, got, before, starts, ends, after)
    plane = lax.all_to_all(chip, XY, 0, 0)

    by_block = kernel.reshape(pairs, 2, taps, width).transpose(2, 0, 1, 3).reshape(blocks, 2, width)
    rows = lax.dynamic_index_in_dim(by_block, jnp.minimum(spot, blocks - 1), 0, keepdims=False)
    packed = call(
        functools.partial(plane_body, depth),
        shape((4, depth, width), BF),
        groups * 2 * depth * width,
        groups * 2 * depth * width * 2,
        0,
        2,
    )(plane, rows)
    act_rows, cot_rows, slope = call(
        functools.partial(prep_body, depth),
        (shape((padded, width), BF), shape((padded, width), BF), shape((length, width), F32)),
        2 * macs,
        8 * length * width * 2,
        1,
        4,
        far=1,
    )(core, x, g, before, after, packed)
    line = lax.all_to_all(packed.transpose(1, 0, 2), "z", 0, 0).transpose(1, 0, 2)
    sent = call(
        functools.partial(line_body, float(groups * section_input.shape[0])),
        shape((groups, 2 * depth + 8, width), BF),
        4 * depth * width,
        groups * 2 * depth * width * 2,
        0,
        1,
        far=1,
    )(line, act_rows)
    own = lax.all_to_all(sent, XY, 0, 0)
    far = lax.ppermute(own, "core", swap)

    near, carry, kernel_grad = call(
        functools.partial(near_body, taps, depth),
        (
            shape((length, half), BF),
            shape((length, width), F32),
            shape((taps, held, width), F32),
        ),
        2 * taps * macs,
        8 * length * width * 2,
        0,
        3,
        [pad, pad],
    )(act_rows, cot_rows, own)
    out, grad = call(
        functools.partial(far_body, taps, depth),
        (shape((length, width), BF), shape((length, width), BF)),
        2 * taps * macs,
        12 * length * width * 2,
        1,
        8,
        [pad, pad],
    )(core, x, g, slope, near, carry, act_rows, cot_rows, far)
    return (out[None], grad[None], kernel_grad.transpose(1, 0, 2))


def solution(mesh):
    seq = mesh.shape["seq"]
    side = int(round(mesh.shape["dp"] ** 0.5))
    fine = Mesh(mesh.devices.reshape(side, side, seq // 2, 2), XY + SEQ)
    return jax.shard_map(
        local,
        mesh=fine,
        in_specs=(P(XY, SEQ, None), P(SEQ, None, None), P(XY, SEQ, None)),
        out_specs=(P(XY, SEQ, None), P(XY, SEQ, None), P(SEQ, None, None)),
        check_vma=False,
    )
```

```python
import functools

import jax
import jax.numpy as jnp
from jax import lax
from jax.experimental import pallas as pl
from jax.experimental.pallas import tpu as pltpu
from jax.sharding import Mesh, PartitionSpec as P

XY = ("x", "y")
SEQ = ("z", "core")
BF = jnp.bfloat16
F32 = jnp.float32
TOP = 8
VMEM_BYTES = 24 * 1024 * 1024


def call(body, out_shape, flops, bytes_accessed, scalars=0, plain=0, scratch=(), far=0):
    specs = [pl.BlockSpec(memory_space=pltpu.SMEM)] * scalars
    specs += [pl.BlockSpec(memory_space=pltpu.VMEM)] * plain
    specs += [pl.BlockSpec(memory_space=pl.ANY)] * far
    outs = jax.tree.map(lambda _: pl.BlockSpec(memory_space=pltpu.VMEM), out_shape)
    return pl.pallas_call(
        body,
        out_shape=out_shape,
        in_specs=specs,
        out_specs=outs,
        scratch_shapes=list(scratch),
        compiler_params=pltpu.CompilerParams(vmem_limit_bytes=VMEM_BYTES),
        cost_estimate=pl.CostEstimate(
            flops=flops, bytes_accessed=bytes_accessed, transcendentals=0
        ),
    )


def norm(rows):
    inputs = rows.astype(F32)
    scale = jnp.sqrt(jnp.mean(inputs * inputs, axis=-1, keepdims=True) + 1e-05)
    return inputs, scale, inputs / scale


def cumulative(values):
    return 0.5 * (1.0 + lax.erf(values * 0.7071067811865476))


def gelu_rows(rows):
    normed = norm(rows)[2]
    return (normed * cumulative(normed)).astype(BF)


def order_rows(core, width, depth):
    half = width // 2
    held = width // (2 * depth)
    j = lax.broadcasted_iota(jnp.int32, (width, 1), 0)
    side = (j >= half).astype(jnp.int32)
    within = j - side * half
    pair = within // (2 * depth)
    member = (within // depth) % 2
    place = within % depth
    source = (place * 2 + (side + core) % 2) * held + 2 * pair + member
    o = lax.broadcasted_iota(jnp.int32, (width, width), 1)
    return jnp.where(o == source, 1.0, 0.0).astype(BF)


def turn(a, b):
    return lax.dot_general(a, b, (((1,), (1,)), ((), ())), preferred_element_type=F32)


def local_grad(act_ref, cot_t, out_ref, pad_ref, taps, pairs):
    length, width = act_ref.shape
    edge = (taps - 1) // 2
    rows = cot_t.shape[0] // pairs
    pad_ref[:TOP] = jnp.zeros((TOP, width), F32)
    pad_ref[TOP : TOP + length] = act_ref[...].astype(F32)
    pad_ref[TOP + length :] = jnp.zeros((TOP, width), F32)
    for shift in range(taps):
        begin = TOP - edge + shift
        window = pad_ref[begin : begin + length].astype(BF)
        part = jnp.dot(cot_t, window, preferred_element_type=F32).astype(out_ref.dtype)
        for i in range(pairs):
            out_ref[shift * pairs + i] = part[i * rows : (i + 1) * rows]


def other_body(
    taps,
    pairs,
    depth,
    core_ref,
    x_ref,
    g_ref,
    out_ref,
    act_ref,
    cot_t_ref,
    starts_ref,
    ends_ref,
    outer_ref,
    pad_ref,
):
    length, width = x_ref.shape
    half = width // 2
    edge = (taps - 1) // 2
    first = [ref[:TOP].astype(F32)[:edge] for ref in (x_ref, g_ref)]
    last = [ref[length - TOP :].astype(F32)[TOP - edge :] for ref in (x_ref, g_ref)]
    first = jnp.concatenate(first, axis=0)
    last = jnp.concatenate(last, axis=0)
    starts_ref[...] = first.astype(BF)
    ends_ref[...] = last.astype(BF)
    left = core_ref[0] == 0
    outer_ref[...] = jnp.where(left, first, last).astype(BF)
    inner = jnp.where(left, last, first)
    rest = jnp.zeros((out_ref.shape[1] - first.shape[0], width), F32)
    out_ref[taps * pairs] = jnp.concatenate([inner, rest], axis=0).astype(BF)
    order = order_rows(core_ref[0], width, depth)
    cot_t_ref[...] = turn(order, g_ref[...]).astype(BF)
    act_ref[...] = gelu_rows(x_ref[...])
    local_grad(act_ref, cot_t_ref[half:], out_ref, pad_ref, taps, pairs)


def mine_body(taps, pairs, act_ref, cot_t_ref, out_ref, pad_ref):
    half = cot_t_ref.shape[0] // 2
    local_grad(act_ref, cot_t_ref[:half], out_ref, pad_ref, taps, pairs)


def pair_body(
    taps,
    depth,
    core_ref,
    mine_ref,
    got_ref,
    outer_ref,
    starts_ref,
    ends_ref,
    out_ref,
    before_ref,
    after_ref,
):
    blocks, rows, width = mine_ref.shape
    edge = (taps - 1) // 2
    pairs = blocks // taps
    half = width // 2
    left = core_ref[0] == 0
    outer = outer_ref[...].astype(F32)
    inner = got_ref[blocks].astype(F32)[: 2 * edge]
    before = jnp.where(left, outer, inner)
    after = jnp.where(left, inner, outer)
    before_ref[...] = before.astype(BF)
    after_ref[...] = after.astype(BF)
    parts = [before, starts_ref[...].astype(F32), ends_ref[...].astype(F32), after]
    act = gelu_rows(jnp.concatenate([p[:edge] for p in parts], axis=0)).astype(F32)
    cot = jnp.concatenate([p[edge:] for p in parts], axis=0).astype(BF)
    order = order_rows(core_ref[0], width, depth)
    cot_t = turn(order, cot)[:half].astype(BF)
    side = 2 * edge
    for shift in range(taps):
        offset = shift - edge
        window = []
        for i in range(2 * side):
            at = i % side
            to = at + offset
            crosses = 0 <= to < side and (at < edge) != (to < edge)
            row = i + offset
            window.append(act[row : row + 1] if crosses else jnp.zeros((1, width), F32))
        extra = jnp.dot(
            cot_t, jnp.concatenate(window, axis=0).astype(BF), preferred_element_type=F32
        )
        for i in range(pairs):
            j = shift * pairs + i
            out_ref[j] = (
                mine_ref[j] + got_ref[j].astype(F32) + extra[i * rows : (i + 1) * rows]
            ).astype(BF)
    for j in range(blocks, out_ref.shape[0]):
        out_ref[j] = jnp.zeros((rows, width), BF)


def plane_body(depth, plane_ref, row_ref, out_ref):
    total = plane_ref[0].astype(F32)
    for i in range(1, plane_ref.shape[0]):
        total = total + plane_ref[i].astype(F32)
    rows = row_ref[...].astype(F32)
    out_ref[0] = jnp.broadcast_to(rows[0:1], out_ref.shape[1:]).astype(BF)
    out_ref[1] = jnp.broadcast_to(rows[1:2], out_ref.shape[1:]).astype(BF)
    out_ref[2] = total[:depth].astype(BF)
    out_ref[3] = total[depth:].astype(BF)


def line_body(share, line_ref, after_ref, out_ref):
    del after_ref
    depth, width = line_ref.shape[1:]
    first = jnp.sum(line_ref[2].astype(F32), axis=0, keepdims=True) / share
    second = jnp.sum(line_ref[3].astype(F32), axis=0, keepdims=True) / share
    both = jnp.concatenate([first, second], axis=0)
    high = both.astype(BF).astype(F32)
    tail = jnp.concatenate([high, both - high, jnp.zeros((4, width), F32)], axis=0).astype(BF)
    for i in range(out_ref.shape[0]):
        out_ref[i, :depth] = line_ref[0]
        out_ref[i, depth : 2 * depth] = line_ref[1]
        out_ref[i, 2 * depth :] = tail


def weight(ref, shift, pairs, rows):
    return jnp.concatenate([ref[shift * pairs + i, :rows] for i in range(pairs)], axis=0)


def prep_body(
    depth,
    core_ref,
    x_ref,
    g_ref,
    before_ref,
    after_ref,
    packed_ref,
    act_ref,
    cot_ref,
    slope_ref,
):
    del packed_ref
    length, width = x_ref.shape
    edge = before_ref.shape[0] // 2
    order = order_rows(core_ref[0], width, depth)
    zeros = jnp.zeros((TOP - edge, width), F32)
    normed = norm(x_ref[...])[2]
    share = cumulative(normed)
    act_ref[TOP : TOP + length] = (normed * share).astype(BF)
    first = gelu_rows(before_ref[:edge]).astype(F32)
    last = gelu_rows(after_ref[:edge]).astype(F32)
    act_ref[:TOP] = jnp.concatenate([zeros, first], axis=0).astype(BF)
    act_ref[TOP + length :] = jnp.concatenate([last, zeros], axis=0).astype(BF)
    cot_ref[TOP : TOP + length] = turn(g_ref[...], order).astype(BF)
    first = turn(before_ref[edge:], order)
    last = turn(after_ref[edge:], order)
    cot_ref[:TOP] = jnp.concatenate([zeros, first], axis=0).astype(BF)
    cot_ref[TOP + length :] = jnp.concatenate([last, zeros], axis=0).astype(BF)
    slope_ref[...] = share + normed * jnp.exp(-0.5 * normed * normed) * 0.3989422804014327


def half_convs(weights, act_pad_ref, cot_pad_ref, side, begin, rows):
    taps = len(weights)
    half, width = weights[0].shape
    edge = (taps - 1) // 2
    at = TOP - edge + begin
    windows = [act_pad_ref[at + shift : at + shift + rows].astype(BF) for shift in range(taps)]
    total = turn(jnp.concatenate(windows, axis=1), jnp.concatenate(weights, axis=1))
    carry = jnp.zeros((rows, width), F32)
    for shift in range(taps):
        back = at + 2 * edge - shift
        window = cot_pad_ref[back : back + rows].astype(BF)[:, side * half : (side + 1) * half]
        carry = carry + jnp.dot(window, weights[shift], preferred_element_type=F32)
    return total.astype(BF), carry


def near_body(
    taps,
    depth,
    act_ref,
    cot_ref,
    own_ref,
    near_ref,
    carry_ref,
    kernel_grad_ref,
    act_pad_ref,
    cot_pad_ref,
):
    length, half = near_ref.shape
    pairs = half // (2 * depth)
    act_pad_ref[...] = act_ref[...].astype(F32)
    cot_pad_ref[...] = cot_ref[...].astype(F32)
    own = [weight(own_ref, shift, pairs, 2 * depth) for shift in range(taps)]
    rows = length // 2
    for begin in range(0, length, rows):
        near_ref[begin : begin + rows], carry_ref[begin : begin + rows] = half_convs(
            own, act_pad_ref, cot_pad_ref, 0, begin, rows
        )
    for shift in range(taps):
        for i in range(pairs):
            value = own_ref[shift * pairs + i, 2 * depth :].astype(F32)
            kernel_grad_ref[shift, 2 * i : 2 * i + 2] = value[:2] + value[2:4]


def far_body(
    taps,
    depth,
    core_ref,
    x_ref,
    g_ref,
    slope_ref,
    near_ref,
    carry_ref,
    act_ref,
    cot_ref,
    far_ref,
    out_ref,
    grad_ref,
    act_pad_ref,
    cot_pad_ref,
):
    length, width = x_ref.shape
    pairs = width // (4 * depth)
    act_pad_ref[...] = act_ref[...].astype(F32)
    cot_pad_ref[...] = cot_ref[...].astype(F32)
    order = order_rows(core_ref[0], width, depth)
    far = [weight(far_ref, shift, pairs, 2 * depth) for shift in range(taps)]
    rows = length // 2
    for begin in range(0, length, rows):
        total, carry = half_convs(far, act_pad_ref, cot_pad_ref, 1, begin, rows)
        carry = carry + carry_ref[begin : begin + rows]
        grouped = jnp.concatenate([near_ref[begin : begin + rows], total], axis=1)
        branch = jnp.dot(grouped, order, preferred_element_type=F32)
        inputs, scale, normed = norm(x_ref[begin : begin + rows])
        out_ref[begin : begin + rows] = (inputs + branch).astype(BF)
        normed_grad = carry * slope_ref[begin : begin + rows]
        project = jnp.mean(normed_grad * normed, axis=-1, keepdims=True)
        grad_ref[begin : begin + rows] = (
            g_ref[begin : begin + rows].astype(F32) + (normed_grad - normed * project) / scale
        ).astype(BF)


def local(section_input, kernel, cotangent):
    x = section_input[0]
    g = cotangent[0]
    length, width = x.shape
    held, taps, _ = kernel.shape
    edge = (taps - 1) // 2
    depth = lax.axis_size("z")
    groups = lax.axis_size(XY)
    count = lax.axis_size(SEQ)
    pairs = held // 2
    blocks = taps * pairs
    half = width // 2
    padded = length + 2 * TOP
    core = lax.axis_index("core").astype(jnp.int32).reshape(1)
    spot = lax.axis_index(XY)
    shape = jax.ShapeDtypeStruct
    swap = [(0, 1), (1, 0)]
    macs = length * width * width

    pad = pltpu.VMEM((padded, width), F32)
    block = (blocks, 2 * depth, width)
    rim = shape((2 * edge, width), BF)
    other, act, cot_t, starts, ends, outer = call(
        functools.partial(other_body, taps, pairs, depth),
        (
            shape((blocks + 1, 2 * depth, width), BF),
            shape((length, width), BF),
            shape((width, length), BF),
            rim,
            rim,
            rim,
        ),
        2 * macs + taps * macs,
        8 * length * width * 2,
        1,
        2,
        [pad],
    )(core, x, g)
    got = lax.ppermute(other, "core", swap)
    across = [(i, i + 1) for i in range(1, count - 1, 2)]
    outer = lax.ppermute(outer, SEQ, across + [(j, i) for i, j in across])
    mine = call(
        functools.partial(mine_body, taps, pairs),
        shape(block, F32),
        taps * macs,
        8 * length * width * 2,
        0,
        2,
        [pad],
    )(act, cot_t)
    chip, before, after = call(
        functools.partial(pair_body, taps, depth),
        (shape((groups, 2 * depth, width), BF), rim, rim),
        taps * half * width,
        taps * half * width * 8,
        1,
        5,
    )(core, mine, got, outer, starts, ends)
    plane = lax.all_to_all(chip, XY, 0, 0)

    by_block = kernel.reshape(pairs, 2, taps, width).transpose(2, 0, 1, 3).reshape(blocks, 2, width)
    rows = lax.dynamic_index_in_dim(by_block, jnp.minimum(spot, blocks - 1), 0, keepdims=False)
    packed = call(
        functools.partial(plane_body, depth),
        shape((4, depth, width), BF),
        groups * 2 * depth * width,
        groups * 2 * depth * width * 2,
        0,
        2,
    )(plane, rows)
    act_rows, cot_rows, slope = call(
        functools.partial(prep_body, depth),
        (shape((padded, width), BF), shape((padded, width), BF), shape((length, width), F32)),
        2 * macs,
        8 * length * width * 2,
        1,
        4,
        far=1,
    )(core, x, g, before, after, packed)
    line = lax.all_to_all(packed.transpose(1, 0, 2), "z", 0, 0).transpose(1, 0, 2)
    sent = call(
        functools.partial(line_body, float(groups * section_input.shape[0])),
        shape((groups, 2 * depth + 8, width), BF),
        4 * depth * width,
        groups * 2 * depth * width * 2,
        0,
        1,
        far=1,
    )(line, act_rows)
    own = lax.all_to_all(sent, XY, 0, 0)
    far = lax.ppermute(own, "core", swap)

    near, carry, kernel_grad = call(
        functools.partial(near_body, taps, depth),
        (
            shape((length, half), BF),
            shape((length, width), F32),
            shape((taps, held, width), F32),
        ),
        2 * taps * macs,
        8 * length * width * 2,
        0,
        3,
        [pad, pad],
    )(act_rows, cot_rows, own)
    out, grad = call(
        functools.partial(far_body, taps, depth),
        (shape((length, width), BF), shape((length, width), BF)),
        2 * taps * macs,
        12 * length * width * 2,
        1,
        8,
        [pad, pad],
    )(core, x, g, slope, near, carry, act_rows, cot_rows, far)
    return (out[None], grad[None], kernel_grad.transpose(1, 0, 2))


def solution(mesh):
    seq = mesh.shape["seq"]
    side = int(round(mesh.shape["dp"] ** 0.5))
    fine = Mesh(mesh.devices.reshape(side, side, seq // 2, 2), XY + SEQ)
    return jax.shard_map(
        local,
        mesh=fine,
        in_specs=(P(XY, SEQ, None), P(SEQ, None, None), P(XY, SEQ, None)),
        out_specs=(P(XY, SEQ, None), P(XY, SEQ, None), P(SEQ, None, None)),
        check_vma=False,
    )
```

```python
import functools

import jax
import jax.numpy as jnp
from jax import lax
from jax.experimental import pallas as pl
from jax.experimental.pallas import tpu as pltpu
from jax.sharding import Mesh, PartitionSpec as P

XY = ("x", "y")
SEQ = ("z", "core")
BF = jnp.bfloat16
F32 = jnp.float32
TOP = 8
VMEM_BYTES = 24 * 1024 * 1024


def call(body, out_shape, flops, bytes_accessed, scalars=0, plain=0, scratch=(), far=0):
    specs = [pl.BlockSpec(memory_space=pltpu.SMEM)] * scalars
    specs += [pl.BlockSpec(memory_space=pltpu.VMEM)] * plain
    specs += [pl.BlockSpec(memory_space=pl.ANY)] * far
    outs = jax.tree.map(lambda _: pl.BlockSpec(memory_space=pltpu.VMEM), out_shape)
    return pl.pallas_call(
        body,
        out_shape=out_shape,
        in_specs=specs,
        out_specs=outs,
        scratch_shapes=list(scratch),
        compiler_params=pltpu.CompilerParams(vmem_limit_bytes=VMEM_BYTES),
        cost_estimate=pl.CostEstimate(
            flops=flops, bytes_accessed=bytes_accessed, transcendentals=0
        ),
    )


def norm(rows):
    inputs = rows.astype(F32)
    scale = jnp.sqrt(jnp.mean(inputs * inputs, axis=-1, keepdims=True) + 1e-05)
    return inputs, scale, inputs / scale


def cumulative(values):
    return 0.5 * (1.0 + lax.erf(values * 0.7071067811865476))


def gelu_rows(rows):
    normed = norm(rows)[2]
    return (normed * cumulative(normed)).astype(BF)


def order_rows(core, width, depth):
    half = width // 2
    held = width // (2 * depth)
    j = lax.broadcasted_iota(jnp.int32, (width, 1), 0)
    side = (j >= half).astype(jnp.int32)
    within = j - side * half
    pair = within // (2 * depth)
    member = (within // depth) % 2
    place = within % depth
    source = (place * 2 + (side + core) % 2) * held + 2 * pair + member
    o = lax.broadcasted_iota(jnp.int32, (width, width), 1)
    return jnp.where(o == source, 1.0, 0.0).astype(BF)


def turn(a, b):
    return lax.dot_general(a, b, (((1,), (1,)), ((), ())), preferred_element_type=F32)


def local_grad(act_ref, cot_t, out_ref, pad_ref, taps, pairs):
    length, width = act_ref.shape
    edge = (taps - 1) // 2
    rows = cot_t.shape[0] // pairs
    pad_ref[:TOP] = jnp.zeros((TOP, width), F32)
    pad_ref[TOP : TOP + length] = act_ref[...].astype(F32)
    pad_ref[TOP + length :] = jnp.zeros((TOP, width), F32)
    for shift in range(taps):
        begin = TOP - edge + shift
        window = pad_ref[begin : begin + length].astype(BF)
        part = jnp.dot(cot_t, window, preferred_element_type=F32).astype(out_ref.dtype)
        for i in range(pairs):
            out_ref[shift * pairs + i] = part[i * rows : (i + 1) * rows]


def other_body(
    taps,
    pairs,
    depth,
    core_ref,
    x_ref,
    g_ref,
    out_ref,
    act_ref,
    cot_t_ref,
    starts_ref,
    ends_ref,
    outer_ref,
    pad_ref,
):
    length, width = x_ref.shape
    half = width // 2
    edge = (taps - 1) // 2
    first = [ref[:TOP].astype(F32)[:edge] for ref in (x_ref, g_ref)]
    last = [ref[length - TOP :].astype(F32)[TOP - edge :] for ref in (x_ref, g_ref)]
    first = jnp.concatenate(first, axis=0)
    last = jnp.concatenate(last, axis=0)
    starts_ref[...] = first.astype(BF)
    ends_ref[...] = last.astype(BF)
    left = core_ref[0] == 0
    outer_ref[...] = jnp.where(left, first, last).astype(BF)
    inner = jnp.where(left, last, first)
    rest = jnp.zeros((out_ref.shape[1] - first.shape[0], width), F32)
    out_ref[taps * pairs] = jnp.concatenate([inner, rest], axis=0).astype(BF)
    order = order_rows(core_ref[0], width, depth)
    cot_t_ref[...] = turn(order, g_ref[...]).astype(BF)
    act_ref[...] = gelu_rows(x_ref[...])
    local_grad(act_ref, cot_t_ref[half:], out_ref, pad_ref, taps, pairs)


def mine_body(taps, pairs, act_ref, cot_t_ref, out_ref, pad_ref):
    half = cot_t_ref.shape[0] // 2
    local_grad(act_ref, cot_t_ref[:half], out_ref, pad_ref, taps, pairs)


def pair_body(
    taps,
    depth,
    core_ref,
    mine_ref,
    got_ref,
    outer_ref,
    starts_ref,
    ends_ref,
    out_ref,
    before_ref,
    after_ref,
):
    blocks, rows, width = mine_ref.shape
    edge = (taps - 1) // 2
    pairs = blocks // taps
    half = width // 2
    left = core_ref[0] == 0
    outer = outer_ref[...].astype(F32)
    inner = got_ref[blocks].astype(F32)[: 2 * edge]
    before = jnp.where(left, outer, inner)
    after = jnp.where(left, inner, outer)
    before_ref[...] = before.astype(BF)
    after_ref[...] = after.astype(BF)
    parts = [before, starts_ref[...].astype(F32), ends_ref[...].astype(F32), after]
    act = gelu_rows(jnp.concatenate([p[:edge] for p in parts], axis=0)).astype(F32)
    cot = jnp.concatenate([p[edge:] for p in parts], axis=0).astype(BF)
    order = order_rows(core_ref[0], width, depth)
    cot_t = turn(order, cot)[:half].astype(BF)
    side = 2 * edge
    for shift in range(taps):
        offset = shift - edge
        window = []
        for i in range(2 * side):
            at = i % side
            to = at + offset
            crosses = 0 <= to < side and (at < edge) != (to < edge)
            row = i + offset
            window.append(act[row : row + 1] if crosses else jnp.zeros((1, width), F32))
        extra = jnp.dot(
            cot_t, jnp.concatenate(window, axis=0).astype(BF), preferred_element_type=F32
        )
        for i in range(pairs):
            j = shift * pairs + i
            out_ref[j] = (
                mine_ref[j] + got_ref[j].astype(F32) + extra[i * rows : (i + 1) * rows]
            ).astype(BF)
    for j in range(blocks, out_ref.shape[0]):
        out_ref[j] = jnp.zeros((rows, width), BF)


def plane_body(depth, plane_ref, row_ref, out_ref):
    total = plane_ref[0].astype(F32)
    for i in range(1, plane_ref.shape[0]):
        total = total + plane_ref[i].astype(F32)
    rows = row_ref[...].astype(F32)
    width = rows.shape[1]
    row_pair = rows.astype(BF).reshape(1, 2, width)
    parts = total.reshape(2, depth, width)
    pair = jnp.stack([parts[0], parts[1]], axis=1).astype(BF)
    out_ref[...] = jnp.concatenate([jnp.broadcast_to(row_pair, (depth, 2, width)), pair], axis=1)


def line_body(share, line_ref, after_ref, out_ref):
    del after_ref
    depth, width = line_ref.shape[1:]
    first = jnp.sum(line_ref[2].astype(F32), axis=0, keepdims=True) / share
    second = jnp.sum(line_ref[3].astype(F32), axis=0, keepdims=True) / share
    both = jnp.concatenate([first, second], axis=0)
    high = both.astype(BF).astype(F32)
    tail = jnp.concatenate([high, both - high, jnp.zeros((4, width), F32)], axis=0).astype(BF)
    for i in range(out_ref.shape[0]):
        out_ref[i, :depth] = line_ref[0]
        out_ref[i, depth : 2 * depth] = line_ref[1]
        out_ref[i, 2 * depth :] = tail


def weight(ref, shift, pairs, rows):
    return jnp.concatenate([ref[shift * pairs + i, :rows] for i in range(pairs)], axis=0)


def prep_body(
    depth,
    core_ref,
    x_ref,
    g_ref,
    before_ref,
    after_ref,
    packed_ref,
    act_ref,
    cot_ref,
    slope_ref,
):
    del packed_ref
    length, width = x_ref.shape
    edge = before_ref.shape[0] // 2
    order = order_rows(core_ref[0], width, depth)
    zeros = jnp.zeros((TOP - edge, width), F32)
    normed = norm(x_ref[...])[2]
    share = cumulative(normed)
    act_ref[TOP : TOP + length] = (normed * share).astype(BF)
    first = gelu_rows(before_ref[:edge]).astype(F32)
    last = gelu_rows(after_ref[:edge]).astype(F32)
    act_ref[:TOP] = jnp.concatenate([zeros, first], axis=0).astype(BF)
    act_ref[TOP + length :] = jnp.concatenate([last, zeros], axis=0).astype(BF)
    cot_ref[TOP : TOP + length] = turn(g_ref[...], order).astype(BF)
    first = turn(before_ref[edge:], order)
    last = turn(after_ref[edge:], order)
    cot_ref[:TOP] = jnp.concatenate([zeros, first], axis=0).astype(BF)
    cot_ref[TOP + length :] = jnp.concatenate([last, zeros], axis=0).astype(BF)
    slope_ref[...] = share + normed * jnp.exp(-0.5 * normed * normed) * 0.3989422804014327


def half_convs(weights, act_pad_ref, cot_pad_ref, side, begin, rows):
    taps = len(weights)
    half, width = weights[0].shape
    edge = (taps - 1) // 2
    at = TOP - edge + begin
    windows = [act_pad_ref[at + shift : at + shift + rows].astype(BF) for shift in range(taps)]
    total = turn(jnp.concatenate(windows, axis=1), jnp.concatenate(weights, axis=1))
    carry = jnp.zeros((rows, width), F32)
    for shift in range(taps):
        back = at + 2 * edge - shift
        window = cot_pad_ref[back : back + rows].astype(BF)[:, side * half : (side + 1) * half]
        carry = carry + jnp.dot(window, weights[shift], preferred_element_type=F32)
    return total.astype(BF), carry


def near_body(
    taps,
    depth,
    act_ref,
    cot_ref,
    own_ref,
    near_ref,
    carry_ref,
    kernel_grad_ref,
    act_pad_ref,
    cot_pad_ref,
):
    length, half = near_ref.shape
    pairs = half // (2 * depth)
    act_pad_ref[...] = act_ref[...].astype(F32)
    cot_pad_ref[...] = cot_ref[...].astype(F32)
    own = [weight(own_ref, shift, pairs, 2 * depth) for shift in range(taps)]
    rows = length // 2
    for begin in range(0, length, rows):
        near_ref[begin : begin + rows], carry_ref[begin : begin + rows] = half_convs(
            own, act_pad_ref, cot_pad_ref, 0, begin, rows
        )
    for shift in range(taps):
        for i in range(pairs):
            value = own_ref[shift * pairs + i, 2 * depth :].astype(F32)
            kernel_grad_ref[shift, 2 * i : 2 * i + 2] = value[:2] + value[2:4]


def far_body(
    taps,
    depth,
    core_ref,
    x_ref,
    g_ref,
    slope_ref,
    near_ref,
    carry_ref,
    act_ref,
    cot_ref,
    far_ref,
    out_ref,
    grad_ref,
    act_pad_ref,
    cot_pad_ref,
):
    length, width = x_ref.shape
    pairs = width // (4 * depth)
    act_pad_ref[...] = act_ref[...].astype(F32)
    cot_pad_ref[...] = cot_ref[...].astype(F32)
    order = order_rows(core_ref[0], width, depth)
    far = [weight(far_ref, shift, pairs, 2 * depth) for shift in range(taps)]
    rows = length // 2
    for begin in range(0, length, rows):
        total, carry = half_convs(far, act_pad_ref, cot_pad_ref, 1, begin, rows)
        carry = carry + carry_ref[begin : begin + rows]
        grouped = jnp.concatenate([near_ref[begin : begin + rows], total], axis=1)
        branch = jnp.dot(grouped, order, preferred_element_type=F32)
        inputs, scale, normed = norm(x_ref[begin : begin + rows])
        out_ref[begin : begin + rows] = (inputs + branch).astype(BF)
        normed_grad = carry * slope_ref[begin : begin + rows]
        project = jnp.mean(normed_grad * normed, axis=-1, keepdims=True)
        grad_ref[begin : begin + rows] = (
            g_ref[begin : begin + rows].astype(F32) + (normed_grad - normed * project) / scale
        ).astype(BF)


def local(section_input, kernel, cotangent):
    x = section_input[0]
    g = cotangent[0]
    length, width = x.shape
    held, taps, _ = kernel.shape
    edge = (taps - 1) // 2
    depth = lax.axis_size("z")
    groups = lax.axis_size(XY)
    count = lax.axis_size(SEQ)
    pairs = held // 2
    blocks = taps * pairs
    half = width // 2
    padded = length + 2 * TOP
    core = lax.axis_index("core").astype(jnp.int32).reshape(1)
    spot = lax.axis_index(XY)
    shape = jax.ShapeDtypeStruct
    swap = [(0, 1), (1, 0)]
    macs = length * width * width

    pad = pltpu.VMEM((padded, width), F32)
    block = (blocks, 2 * depth, width)
    rim = shape((2 * edge, width), BF)
    other, act, cot_t, starts, ends, outer = call(
        functools.partial(other_body, taps, pairs, depth),
        (
            shape((blocks + 1, 2 * depth, width), BF),
            shape((length, width), BF),
            shape((width, length), BF),
            rim,
            rim,
            rim,
        ),
        2 * macs + taps * macs,
        8 * length * width * 2,
        1,
        2,
        [pad],
    )(core, x, g)
    got = lax.ppermute(other, "core", swap)
    across = [(i, i + 1) for i in range(1, count - 1, 2)]
    outer = lax.ppermute(outer, SEQ, across + [(j, i) for i, j in across])
    mine = call(
        functools.partial(mine_body, taps, pairs),
        shape(block, F32),
        taps * macs,
        8 * length * width * 2,
        0,
        2,
        [pad],
    )(act, cot_t)
    chip, before, after = call(
        functools.partial(pair_body, taps, depth),
        (shape((groups, 2 * depth, width), BF), rim, rim),
        taps * half * width,
        taps * half * width * 8,
        1,
        5,
    )(core, mine, got, outer, starts, ends)
    plane = lax.all_to_all(chip, XY, 0, 0)

    by_block = kernel.reshape(pairs, 2, taps, width).transpose(2, 0, 1, 3).reshape(blocks, 2, width)
    rows = lax.dynamic_index_in_dim(by_block, jnp.minimum(spot, blocks - 1), 0, keepdims=False)
    packed = call(
        functools.partial(plane_body, depth),
        shape((depth, 4, width), BF),
        groups * 2 * depth * width,
        groups * 2 * depth * width * 2,
        0,
        2,
    )(plane, rows)
    act_rows, cot_rows, slope = call(
        functools.partial(prep_body, depth),
        (shape((padded, width), BF), shape((padded, width), BF), shape((length, width), F32)),
        2 * macs,
        8 * length * width * 2,
        1,
        4,
        far=1,
    )(core, x, g, before, after, packed)
    line = lax.all_to_all(packed, "z", 0, 0).transpose(1, 0, 2)
    sent = call(
        functools.partial(line_body, float(groups * section_input.shape[0])),
        shape((groups, 2 * depth + 8, width), BF),
        4 * depth * width,
        groups * 2 * depth * width * 2,
        0,
        1,
        far=1,
    )(line, act_rows)
    own = lax.all_to_all(sent, XY, 0, 0)
    far = lax.ppermute(own, "core", swap)

    near, carry, kernel_grad = call(
        functools.partial(near_body, taps, depth),
        (
            shape((length, half), BF),
            shape((length, width), F32),
            shape((taps, held, width), F32),
        ),
        2 * taps * macs,
        8 * length * width * 2,
        0,
        3,
        [pad, pad],
    )(act_rows, cot_rows, own)
    out, grad = call(
        functools.partial(far_body, taps, depth),
        (shape((length, width), BF), shape((length, width), BF)),
        2 * taps * macs,
        12 * length * width * 2,
        1,
        8,
        [pad, pad],
    )(core, x, g, slope, near, carry, act_rows, cot_rows, far)
    return (out[None], grad[None], kernel_grad.transpose(1, 0, 2))


def solution(mesh):
    seq = mesh.shape["seq"]
    side = int(round(mesh.shape["dp"] ** 0.5))
    fine = Mesh(mesh.devices.reshape(side, side, seq // 2, 2), XY + SEQ)
    return jax.shard_map(
        local,
        mesh=fine,
        in_specs=(P(XY, SEQ, None), P(SEQ, None, None), P(XY, SEQ, None)),
        out_specs=(P(XY, SEQ, None), P(XY, SEQ, None), P(SEQ, None, None)),
        check_vma=False,
    )
```
